32 devices in a mesh: groups: 2 (over y), tm: 16 (over z, x, core).
Axes of the slice: x: 2, y: 2, z: 4, core: 2. Of those that a mesh axis runs over, the one named last changes fastest.
Arguments:
- features: bfloat16 [131072, 256], P(('groups', 'tm')), parts along dimension 0, may hold values from -6 to 6
- segment: int32 [131072], P(('groups', 'tm')), parts along dimension 0, may hold values from 0 to 63, never falling along the last dimension, each value on 1 to 8192 neighbouring positions
- w_first: bfloat16 [768, 256], replicated, may hold values from -0.21875 to 0.21875
- w_second: bfloat16 [768, 256], replicated, may hold values from -0.21875 to 0.21875
- w_head: bfloat16 [256, 32], replicated, may hold values from -0.375 to 0.375
- targets: float32 [131072, 32], P(('groups', 'tm')), parts along dimension 0, may hold values from -6 to 6
Outputs:
- hidden: bfloat16 [131072, 256], P(('groups', 'tm')), parts along dimension 0
- grad_features: bfloat16 [131072, 256], P(('groups', 'tm')), parts along dimension 0
- grad_first: float32 [1536, 256], P('groups'), parts along dimension 0
- grad_second: float32 [1536, 256], P('groups'), parts along dimension 0
- grad_head: float32 [512, 32], P('groups'), parts along dimension 0
- loss: float32 [2], P('groups'), parts along dimension 0
The draws below stay inside these ranges and needn't reach their ends.
There are 2 independent parts, one for each index of `groups`. The reference program is written for one: setup_inputs(seed, part) draws one part's arguments, and reference() takes and returns one part's arrays. A program takes and returns all parts, laid end to end along the dimension named above; an argument that names none is the same for every part. Nothing has to cross between parts.
Inputs may be any that keep to these rules, and one draw needn't show every extreme that they name: Segment numbers never fall along time; each segment covers 1 to 8192 samples, one exactly 8192.
All inputs are finite; a program needn't handle non-finite values.
Results may differ from the reference program's by a relative error of at most 0.0075.
Values may be sent and summed in bfloat16 or wider, within the bound.
A program may use at most 128 MiB of HBM per device.

```python
import math
import jax
import jax.numpy as jnp
import numpy as np

CH = 256
TRAITS = 32
D_FIRST = 4
D_SECOND = 16
TIME = 65536
SEGS = 64
SEG_MOST = 8192


def block_scale(key, dims, cuts, least, largest):
    gain = 1.0
    for position, shards_of in cuts:
        draws = jax.random.uniform(jax.random.fold_in(jax.random.fold_in(key, 6), position), (shards_of,), jnp.float32, least / len(cuts), largest / len(cuts))
        gain = gain * jnp.repeat(jnp.exp(draws), dims[position] // shards_of).reshape((-1,) + (1,) * (len(dims) - 1 - position))
    return gain


def profile(number_of, total, reach, skew):
    weights = [(1 << 20) // math.isqrt(standing ** skew) + 1 for standing in range(2, number_of + 1)]
    spare, given = total - reach - (number_of - 1), [1] * (number_of - 1)
    while spare > 0:
        movable = [i for i in range(number_of - 1) if given[i] < reach]
        mass, left = sum([weights[i] for i in movable]), spare
        for i in movable:
            extra = min(reach - given[i], max(1, left * weights[i] // mass), spare)
            given[i] = given[i] + extra
            spare = spare - extra
    return np.array([reach] + given)


def uneven(stream_key, number_of, total, bound, slope):
    if number_of == 2:
        one = jax.random.randint(stream_key, (), max(1, total - bound), min(bound, total - 1) + 1)
        return jnp.stack([one, total - one])
    tallies = jnp.asarray(profile(number_of, total, bound, slope), jnp.int32)
    pairs = (number_of - 1) // 2
    donor, receiver = tallies[1:1 + 2 * pairs:2], tallies[2:2 + 2 * pairs:2]
    room = jnp.minimum(donor - 1, bound - receiver)
    passed = jax.random.randint(jax.random.fold_in(stream_key, 1), (pairs,), 0, 1 << 20) % (room + 1)
    tallies = tallies.at[1:1 + 2 * pairs:2].set(donor - passed).at[2:2 + 2 * pairs:2].set(receiver + passed)
    return tallies[jax.random.permutation(jax.random.fold_in(stream_key, 2), number_of)]


def gaussian(stream_key, extent, spread, limit, split=(), kind=jnp.bfloat16):
    loudness = block_scale(stream_key, extent, split, -0.22, 0.18) if split else 1.0
    entries = jax.random.normal(stream_key, extent, jnp.float32) * spread * loudness
    return jnp.minimum(jnp.maximum(entries, -limit), limit).astype(kind)


def setup_inputs(seed: int = 0, part: int = 0) -> dict:
    seeds = jax.random.split(jax.random.key(seed), 7)
    part_splits = jax.random.split(jax.random.fold_in(seeds[6], part), 7)
    features = gaussian(part_splits[0], (TIME, CH), 1.0, 6.0, ((0, 16),))
    segment = jnp.searchsorted(jnp.cumsum(uneven(part_splits[1], SEGS, TIME, SEG_MOST, 2)), jnp.arange(TIME), side="right").astype(jnp.int32)
    w_first = gaussian(seeds[2], (3 * CH, CH), (3 * CH) ** -0.5, 0.21875)
    w_second = gaussian(seeds[3], (3 * CH, CH), (3 * CH) ** -0.5, 0.21875)
    w_head = gaussian(seeds[4], (CH, TRAITS), CH ** -0.5, 0.375)
    targets = gaussian(part_splits[5], (TIME, TRAITS), 1.0, 6.0, ((0, 16),), jnp.float32)
    return dict(features=features, segment=segment, w_first=w_first, w_second=w_second, w_head=w_head, targets=targets)


def tap_stack(padded, seg_pad, margin, dilation, rows):
    center = seg_pad[margin:margin + rows]
    pieces = []
    for tap in range(3):
        start = margin + (tap - 1) * dilation
        keep = (seg_pad[start:start + rows] == center)[:, None]
        pieces.append(jnp.where(keep, padded[start:start + rows], jnp.zeros((), padded.dtype)))
    return jnp.concatenate(pieces, 1)


def back_stack(padded, seg_pad, margin, dilation, rows):
    center = seg_pad[margin:margin + rows]
    pieces = []
    for tap in range(3):
        start = margin - (tap - 1) * dilation
        keep = (seg_pad[start:start + rows] == center)[:, None]
        pieces.append(jnp.where(keep, padded[start:start + rows], jnp.zeros((), padded.dtype)))
    return jnp.concatenate(pieces, 1)


def flipped(weight):
    width = weight.shape[1]
    return jnp.swapaxes(weight.reshape(3, width, width), 1, 2).reshape(3 * width, width)


def reference(features, segment, w_first, w_second, w_head, targets):
    margin = D_FIRST + D_SECOND
    seg_pad = jnp.pad(segment + 1, (margin, margin))

    def padrows(field):
        return jnp.pad(field, ((margin, margin), (0, 0)))

    first_in = tap_stack(padrows(features), seg_pad, margin, D_FIRST, TIME)
    pre_first = jnp.dot(first_in, w_first, preferred_element_type=jnp.float32)
    act_first = jnp.maximum(pre_first, 0.0).astype(jnp.bfloat16)
    second_in = tap_stack(padrows(act_first), seg_pad, margin, D_SECOND, TIME)
    pre_second = jnp.dot(second_in, w_second, preferred_element_type=jnp.float32)
    hidden = (features.astype(jnp.float32) + pre_second).astype(jnp.bfloat16)
    error = jnp.dot(hidden, w_head, preferred_element_type=jnp.float32) - targets
    loss = jnp.sum(error * error) / (TIME * TRAITS)
    scale = 1.0 / (TIME ** 0.5)
    grad_out = (error * scale).astype(jnp.bfloat16)
    grad_head = jnp.dot(hidden.T, grad_out, preferred_element_type=jnp.float32)
    grad_hidden = jnp.dot(grad_out, w_head.T, preferred_element_type=jnp.float32)
    grad_pre2 = grad_hidden.astype(jnp.bfloat16)
    grad_second = jnp.dot(second_in.T, grad_pre2, preferred_element_type=jnp.float32)
    grad_act = jnp.dot(back_stack(padrows(grad_pre2), seg_pad, margin, D_SECOND, TIME), flipped(w_second), preferred_element_type=jnp.float32)
    grad_pre1 = jnp.where(pre_first > 0, grad_act, 0.0).astype(jnp.bfloat16)
    grad_first = jnp.dot(first_in.T, grad_pre1, preferred_element_type=jnp.float32)
    grad_features = grad_hidden + jnp.dot(back_stack(padrows(grad_pre1), seg_pad, margin, D_FIRST, TIME), flipped(w_first), preferred_element_type=jnp.float32)
    return hidden, grad_features.astype(jnp.bfloat16), grad_first, grad_second, grad_head, jnp.reshape(loss, (1,))
```

```python
import functools

import jax
import jax.numpy as jnp
from jax import lax
from jax.experimental import pallas as pl
from jax.experimental.pallas import tpu as pltpu
from jax.sharding import PartitionSpec as P

D_FIRST = 4
D_SECOND = 16
EDGE = 128
GAP = 16
BASE = EDGE + GAP
HALO = 64
BF, F32 = jnp.bfloat16, jnp.float32
MESH = pl.DeviceIdType.MESH


def dot(a, b, ca=1, cb=0):
    return lax.dot_general(a, b, (((ca,), (cb,)), ((), ())), preferred_element_type=F32)


def compute(rows, scale, feat, flo, fhi, seg, tgt, tlo, thi, w1, w2, wht,
            hid, gfeat, g1, g2, gh, err,
            fb, f32, segc, msk, act, gp2, gp1, ghid, w1t, w2t, ght, sem):
    ch = w1.shape[1]
    total = rows + 2 * BASE
    step = min(512, rows)
    steps = rows // step

    copies = [
        pltpu.make_async_copy(feat, fb.at[pl.ds(BASE, rows)], sem.at[0]),
        pltpu.make_async_copy(flo, fb.at[pl.ds(BASE - HALO, HALO)], sem.at[1]),
        pltpu.make_async_copy(fhi, fb.at[pl.ds(BASE + rows, HALO)], sem.at[2]),
    ]
    for copy in copies:
        copy.start()

    diagonal = lax.broadcasted_iota(jnp.int32, (128, 128), 0) == lax.broadcasted_iota(
        jnp.int32, (128, 128), 1)
    ones = jnp.ones((256, 128), BF)

    def column(i, _):
        row = jnp.broadcast_to(seg[pl.ds(i, 1), :], (128, 128))
        low = row & 255
        high = row - low
        both = jnp.concatenate([jnp.where(diagonal, low, 0), jnp.where(diagonal, high, 0)], 1)
        segc[pl.ds(pl.multiple_of(GAP + i * 128, 16), 128), :] = dot(both.astype(F32).astype(BF), ones)
        return 0

    lax.fori_loop(0, seg.shape[0], column, 0)
    segc[0:GAP, :] = jnp.full((GAP, 128), -1.0, F32)
    segc[total - GAP:total, :] = jnp.full((GAP, 128), -1.0, F32)

    def masks(i, _):
        q = pl.multiple_of(GAP + i * 128, 16)
        around = segc.at[pl.ds(q - GAP, 128 + 2 * GAP), :]
        center = around[GAP:GAP + 128, :]
        for n, off in enumerate((-D_FIRST, D_FIRST, -D_SECOND, D_SECOND)):
            same = around[GAP + off:GAP + off + 128, :] == center
            msk[n, pl.ds(q, 128), :] = jnp.where(same, 1.0, 0.0).astype(BF)
        return 0

    lax.fori_loop(0, seg.shape[0], masks, 0)

    for k in range(3):
        w1t[k * ch:(k + 1) * ch, :] = w1[k * ch:(k + 1) * ch, :].T
        w2t[k * ch:(k + 1) * ch, :] = w2[k * ch:(k + 1) * ch, :].T
    for scratch, edge, kind in ((act, GAP, BF), (gp2, GAP, BF), (fb, BASE - HALO, BF), (gp1, EDGE, F32)):
        zero = jnp.zeros((edge, ch), kind)
        scratch[0:edge, :] = zero
        scratch[total - edge:total, :] = zero
    g1[...] = jnp.zeros_like(g1)
    g2[...] = jnp.zeros_like(g2)
    ght[...] = jnp.zeros_like(ght)
    err[...] = jnp.zeros_like(err)
    for copy in copies:
        copy.wait()

    def widen(q, size):
        f32[pl.ds(q, size), :] = fb[pl.ds(q, size), :].astype(F32)

    def mask(n, q, size):
        m = msk[n, pl.ds(q, size), :]
        return jnp.concatenate([m] * (ch // 128), 1)

    def near(wide, exact, q, size, back):
        around = wide.at[pl.ds(q - 8, size + 16), :]
        sides = (around[8 - D_FIRST:8 - D_FIRST + size, :].astype(BF) * mask(0, q, size),
                 around[8 + D_FIRST:8 + D_FIRST + size, :].astype(BF) * mask(1, q, size))
        low, high = sides[::-1] if back else sides
        return jnp.concatenate([low, exact, high], 1)

    def far(field, q, size, back):
        sides = (field[pl.ds(q - D_SECOND, size), :] * mask(2, q, size),
                 field[pl.ds(q + D_SECOND, size), :] * mask(3, q, size))
        low, high = sides[::-1] if back else sides
        return jnp.concatenate([low, field[pl.ds(q, size), :], high], 1)

    def first(q, size):
        x = near(f32, fb[pl.ds(q, size), :], q, size, False)
        act[pl.ds(q, size), :] = jnp.maximum(dot(x, w1[...]), 0.0).astype(BF)

    def second(q, size, targets):
        y = far(act, q, size, False)
        h = (f32[pl.ds(q, size), :] + dot(y, w2[...])).astype(BF)
        error = dot(wht[...], h, 1, 1) - targets
        gout = (error * scale).astype(BF)
        back = dot(gout, wht[...], 0, 0)
        gp2[pl.ds(q, size), :] = back.astype(BF)
        return h, error, gout, back

    def own(i):
        return (pl.multiple_of(i * step, step), pl.multiple_of(BASE + i * step, 16))

    def loop(body):
        lax.fori_loop(0, steps, lambda i, c: (body(*own(i)), c)[1], 0)

    last = BASE + rows
    widen(0, BASE)
    widen(last, BASE)
    loop(lambda t, q: widen(q, step))
    first(GAP, EDGE)
    first(last, EDGE)
    loop(lambda t, q: first(q, step))

    second(GAP, EDGE, tlo[...])
    second(last, EDGE, thi[...])

    def middle(t, q):
        h, error, gout, back = second(q, step, tgt[:, pl.ds(t, step)])
        hid[pl.ds(t, step), :] = h
        ghid[pl.ds(t, step), :] = back
        square = error * error
        part = square[:, 0:128]
        for j in range(1, step // 128):
            part = part + square[:, j * 128:(j + 1) * 128]
        err[...] += part
        ght[0:32, :] += dot(gout, h)

    loop(middle)

    def third(q, size):
        b = far(gp2, q, size, True)
        a = act[pl.ds(q, size), :]
        g = jnp.where(a > 0, dot(b, w2t[...]), 0.0)
        gp1[pl.ds(q, size), :] = g.astype(BF).astype(F32)
        return a, b

    third(EDGE, GAP)
    third(last, GAP)

    def outer(t, q):
        a, b = third(q, step)
        g2[...] += dot(a, b, 0, 0)

    loop(outer)

    def final(t, q):
        b = near(gp1, gp1[pl.ds(q, step), :].astype(BF), q, step, True)
        g1[...] += dot(fb[pl.ds(q, step), :], b, 0, 0)
        gfeat[pl.ds(t, step), :] = (ghid[pl.ds(t, step), :] + dot(b, w1t[...])).astype(BF)

    loop(final)
    gh[...] = ght[...].T


def local(features, flo, fhi, seg, tgt, tlo, thi, w_first, w_second, wht, scale):
    rows, ch = features.shape
    total = rows + 2 * BASE
    vmem = pl.BlockSpec(memory_space=pltpu.VMEM)
    anys = pl.BlockSpec(memory_space=pl.ANY)
    traits = wht.shape[0]
    flops = 2 * rows * ch * ch * 20
    return pl.pallas_call(
        functools.partial(compute, rows, scale),
        out_shape=[
            jax.ShapeDtypeStruct((rows, ch), BF),
            jax.ShapeDtypeStruct((rows, ch), BF),
            jax.ShapeDtypeStruct((ch, 3 * ch), F32),
            jax.ShapeDtypeStruct((ch, 3 * ch), F32),
            jax.ShapeDtypeStruct((ch, 128), F32),
            jax.ShapeDtypeStruct((traits, 128), F32),
        ],
        in_specs=[anys] * 3 + [vmem] * 7,
        out_specs=[vmem] * 6,
        scratch_shapes=[
            pltpu.VMEM((total, ch), BF),
            pltpu.VMEM((total, ch), F32),
            pltpu.VMEM((total, 128), F32),
            pltpu.VMEM((4, total, 128), BF),
            pltpu.VMEM((total, ch), BF),
            pltpu.VMEM((total, ch), BF),
            pltpu.VMEM((total, ch), F32),
            pltpu.VMEM((rows, ch), F32),
            pltpu.VMEM((3 * ch, ch), BF),
            pltpu.VMEM((3 * ch, ch), BF),
            pltpu.VMEM((128, ch), F32),
            pltpu.SemaphoreType.DMA((3,)),
        ],
        compiler_params=pltpu.CompilerParams(vmem_limit_bytes=56 * 2**20),
        cost_estimate=pl.CostEstimate(flops=flops, bytes_accessed=8 * rows * ch, transcendentals=0),
    )(features, flo, fhi, seg, tgt, tlo, thi, w_first, w_second, wht)


def total_kernel(g1, g2, gh, err, o1, o2, oh, oe,
                 out1, in1, part1, out2, in2, part2, in3, out3, res, eout, ein, ez, ssem, rsem):
    me = lax.axis_index("tm")
    group = lax.axis_index("groups")
    core, x, z = lax.rem(me, 2), lax.rem(me // 2, 2), me // 4

    def at(zz, xx, cc):
        return (group, (zz * 2 + xx) * 2 + cc)

    other_core = at(z, x, 1 - core)
    other_x = at(z, 1 - x, core)
    others_z = [at(lax.rem(z + k, 4), x, core) for k in (1, 2, 3)]

    barrier = pltpu.get_barrier_semaphore()
    for peer in [other_core, other_x] + others_z:
        pl.semaphore_signal(barrier, inc=1, device_id=peer, device_id_type=MESH)
    pl.semaphore_wait(barrier, 5)

    count = [0]

    def send(src, dst, peer):
        n = count[0]
        count[0] += 1
        copy = pltpu.make_async_remote_copy(
            src_ref=src, dst_ref=dst, send_sem=ssem.at[n], recv_sem=rsem.at[n],
            device_id=peer, device_id_type=MESH)
        copy.start()
        return copy

    sent = []
    wide = g2.shape[1]
    half, quarter, mine = 128, 64, 16
    c0 = pl.multiple_of(core * half, half)
    c1 = pl.multiple_of((1 - core) * half, half)
    x0 = pl.multiple_of(x * quarter, quarter)
    x1 = pl.multiple_of((1 - x) * quarter, quarter)
    z0 = pl.multiple_of(z * mine, mine)

    pieces = [(0, wide), (wide, wide + 128)]

    def load(piece, start):
        if piece == 0:
            return g2[pl.ds(start, half), :]
        return jnp.concatenate([g1[pl.ds(start, half), :], gh[pl.ds(start, half), :]], 1)

    def cols(ref, piece):
        start, size = pieces[piece]
        return ref.at[:, start:start + size]

    def step1(p):
        start, size = pieces[p]
        out1[:, start:start + size] = load(p, c1).astype(BF)
        return send(cols(out1, p), cols(in1, p), other_core)

    def step2(p):
        start, size = pieces[p]
        part1[:, start:start + size] = load(p, c0) + in1[:, start:start + size].astype(F32)
        out2[:, start:start + size] = part1[pl.ds(x1, quarter), start:start + size].astype(BF)
        return send(cols(out2, p), cols(in2, p), other_x)

    def step3(p):
        start, size = pieces[p]
        part2[:, start:start + size] = (
            part1[pl.ds(x0, quarter), start:start + size] + in2[:, start:start + size].astype(F32))
        out3[:, start:start + size] = part2[:, start:start + size].astype(BF)
        copies = []
        for k in (1, 2, 3):
            to = pl.multiple_of(lax.rem(z + k, 4) * mine, mine)
            copies.append(send(out3.at[pl.ds(to, mine), start:start + size],
                               in3.at[k - 1, :, start:start + size], others_z[k - 1]))
        return copies

    home = pl.multiple_of(c0 + x0 + z0, mine)
    home_x = pl.multiple_of(c0 + x0, quarter)

    def step4(p):
        start, size = pieces[p]
        total = part2[pl.ds(z0, mine), start:start + size]
        for k in range(3):
            total = total + in3[k, :, start:start + size].astype(F32)
        res[pl.ds(home, mine), start:start + size] = total.astype(BF)
        spot = res.at[pl.ds(home, mine), start:start + size]
        return [send(spot, spot, others_z[k]) for k in range(3)]

    def step5(p):
        start, size = pieces[p]
        spot = res.at[pl.ds(home_x, quarter), start:start + size]
        return send(spot, spot, other_x)

    def step6(p):
        start, size = pieces[p]
        spot = res.at[pl.ds(c0, half), start:start + size]
        return send(spot, spot, other_core)

    def arrived(copies):
        for copy in copies if isinstance(copies, list) else [copies]:
            copy.wait()

    eout[0] = err[...]
    flying = [step1(0), step1(1)]
    error = send(eout.at[0], ein.at[0], other_core)
    for number, step in enumerate((step2, step3, step4, step5, step6)):
        for p in range(2):
            arrived(flying[p])
            flying[p] = step(p)
        if number == 0:
            error.wait()
            eout[1] = eout[0] + ein[0]
            error = send(eout.at[1], ein.at[1], other_x)
        elif number == 1:
            error.wait()
            ez[z] = eout[1] + ein[1]
            error = [send(ez.at[z], ez.at[z], peer) for peer in others_z]
        elif number == 2:
            arrived(error)
            oe[...] = ez[0] + ez[1] + ez[2] + ez[3]

    arrived(flying[0])
    o2[...] = res[:, 0:wide].astype(F32)
    arrived(flying[1])
    o1[...] = res[:, wide:2 * wide].astype(F32)
    oh[...] = res[:, 2 * wide:].astype(F32).T


def summed(g1, g2, gh, err):
    ch, wide = g1.shape
    every = 2 * wide + 128
    vmem = pl.BlockSpec(memory_space=pltpu.VMEM)
    return pl.pallas_call(
        total_kernel,
        out_shape=[
            jax.ShapeDtypeStruct((ch, wide), F32),
            jax.ShapeDtypeStruct((ch, wide), F32),
            jax.ShapeDtypeStruct((128, ch), F32),
            jax.ShapeDtypeStruct(err.shape, F32),
        ],
        in_specs=[vmem] * 4,
        out_specs=[vmem] * 4,
        scratch_shapes=[
            pltpu.VMEM((128, every), BF), pltpu.VMEM((128, every), BF), pltpu.VMEM((128, every), F32),
            pltpu.VMEM((64, every), BF), pltpu.VMEM((64, every), BF), pltpu.VMEM((64, every), F32),
            pltpu.VMEM((3, 16, every), BF), pltpu.VMEM((64, every), BF), pltpu.VMEM((ch, every), BF),
            pltpu.VMEM((2,) + err.shape, F32), pltpu.VMEM((2,) + err.shape, F32),
            pltpu.VMEM((4,) + err.shape, F32),
            pltpu.SemaphoreType.DMA((25,)), pltpu.SemaphoreType.DMA((25,)),
        ],
        compiler_params=pltpu.CompilerParams(
            collective_id=1, has_side_effects=True, vmem_limit_bytes=32 * 2**20),
    )(g1, g2, gh, err)


def around(cells, dim, width):
    count = lax.axis_size("tm")
    head = lax.slice_in_dim(cells, 0, width, axis=dim)
    tail = lax.slice_in_dim(cells, cells.shape[dim] - width, cells.shape[dim], axis=dim)
    return (lax.ppermute(tail, "tm", [(i, i + 1) for i in range(count - 1)]),
            lax.ppermute(head, "tm", [(i + 1, i) for i in range(count - 1)]))


def shards(features, segment, w_first, w_second, w_head, targets):
    rows, ch = features.shape
    count = lax.axis_size("tm")
    every = rows * count
    traits = w_head.shape[1]
    tgt, wht = targets.T, w_head.T
    flo, fhi = around(features, 0, HALO)
    slo, shi = around(segment + 1, 0, EDGE)
    tlo, thi = around(tgt, 1, EDGE)
    seg = jnp.concatenate([slo, segment + 1, shi]).reshape(-1, 128)
    hidden, gfeat, g1, g2, gh, err = local(
        features, flo, fhi, seg, tgt, tlo, thi, w_first, w_second, wht, 1.0 / every**0.5)
    if count == 16 and ch == 256:
        g1, g2, ght, err = summed(g1, g2, gh, err)
    else:
        g1, g2, gh, err = lax.psum((g1, g2, gh, err), "tm")
        ght = gh.T
    loss = jnp.reshape(jnp.sum(err) / (every * traits), (1,))

    def taps(g):
        return jnp.concatenate([g[:, k * ch:(k + 1) * ch] for k in range(3)], 0)

    return hidden, gfeat, taps(g1), taps(g2), ght[:traits].T, loss


def solution(mesh):
    return jax.shard_map(
        shards,
        mesh=mesh,
        in_specs=(
            P(("groups", "tm"), None),
            P(("groups", "tm")),
            P(),
            P(),
            P(),
            P(("groups", "tm"), None),
        ),
        out_specs=(
            P(("groups", "tm"), None),
            P(("groups", "tm"), None),
            P("groups", None),
            P("groups", None),
            P("groups", None),
            P("groups"),
        ),
        check_vma=False,
    )
```

```python
import functools

import jax
import jax.numpy as jnp
from jax import lax
from jax.experimental import pallas as pl
from jax.experimental.pallas import tpu as pltpu
from jax.sharding import PartitionSpec as P

D_FIRST = 4
D_SECOND = 16
EDGE = 128
GAP = 16
BASE = EDGE + GAP
HALO = 64
BF, F32 = jnp.bfloat16, jnp.float32
MESH = pl.DeviceIdType.MESH


def dot(a, b, ca=1, cb=0):
    return lax.dot_general(a, b, (((ca,), (cb,)), ((), ())), preferred_element_type=F32)


def compute(rows, scale, feat, flo, fhi, seg, tgt, tlo, thi, w1, w2, wht,
            hid, gfeat, g1, g2, gh, err,
            fb, f32, segc, msk, act, gp2, gp1, ghid, w1t, w2t, ght, hids, gfs, sem):
    ch = w1.shape[1]
    total = rows + 2 * BASE
    step = min(512, rows)
    steps = rows // step

    copies = [
        pltpu.make_async_copy(feat, fb.at[pl.ds(BASE, rows)], sem.at[0]),
        pltpu.make_async_copy(flo, fb.at[pl.ds(BASE - HALO, HALO)], sem.at[1]),
        pltpu.make_async_copy(fhi, fb.at[pl.ds(BASE + rows, HALO)], sem.at[2]),
    ]
    for copy in copies:
        copy.start()

    diagonal = lax.broadcasted_iota(jnp.int32, (128, 128), 0) == lax.broadcasted_iota(
        jnp.int32, (128, 128), 1)
    ones = jnp.ones((256, 128), BF)

    def column(i, _):
        row = jnp.broadcast_to(seg[pl.ds(i, 1), :], (128, 128))
        low = row & 255
        high = row - low
        both = jnp.concatenate([jnp.where(diagonal, low, 0), jnp.where(diagonal, high, 0)], 1)
        segc[pl.ds(pl.multiple_of(GAP + i * 128, 16), 128), :] = dot(both.astype(F32).astype(BF), ones)
        return 0

    lax.fori_loop(0, seg.shape[0], column, 0)
    segc[0:GAP, :] = jnp.full((GAP, 128), -1.0, F32)
    segc[total - GAP:total, :] = jnp.full((GAP, 128), -1.0, F32)

    def masks(i, _):
        q = pl.multiple_of(GAP + i * 128, 16)
        around = segc.at[pl.ds(q - GAP, 128 + 2 * GAP), :]
        center = around[GAP:GAP + 128, :]
        for n, off in enumerate((-D_FIRST, D_FIRST, -D_SECOND, D_SECOND)):
            same = around[GAP + off:GAP + off + 128, :] == center
            msk[n, pl.ds(q, 128), :] = jnp.where(same, 1.0, 0.0).astype(BF)
        return 0

    lax.fori_loop(0, seg.shape[0], masks, 0)

    for k in range(3):
        w1t[k * ch:(k + 1) * ch, :] = w1[k * ch:(k + 1) * ch, :].T
        w2t[k * ch:(k + 1) * ch, :] = w2[k * ch:(k + 1) * ch, :].T
    for scratch, edge, kind in ((act, GAP, BF), (gp2, GAP, BF), (fb, BASE - HALO, BF), (gp1, EDGE, F32)):
        zero = jnp.zeros((edge, ch), kind)
        scratch[0:edge, :] = zero
        scratch[total - edge:total, :] = zero
    g1[...] = jnp.zeros_like(g1)
    g2[...] = jnp.zeros_like(g2)
    ght[...] = jnp.zeros_like(ght)
    err[...] = jnp.zeros_like(err)
    for copy in copies:
        copy.wait()

    def widen(q, size):
        f32[pl.ds(q, size), :] = fb[pl.ds(q, size), :].astype(F32)

    def mask(n, q, size):
        m = msk[n, pl.ds(q, size), :]
        return jnp.concatenate([m] * (ch // 128), 1)

    def near(wide, exact, q, size, back):
        around = wide.at[pl.ds(q - 8, size + 16), :]
        sides = (around[8 - D_FIRST:8 - D_FIRST + size, :].astype(BF) * mask(0, q, size),
                 around[8 + D_FIRST:8 + D_FIRST + size, :].astype(BF) * mask(1, q, size))
        low, high = sides[::-1] if back else sides
        return jnp.concatenate([low, exact, high], 1)

    def far(field, q, size, back):
        sides = (field[pl.ds(q - D_SECOND, size), :] * mask(2, q, size),
                 field[pl.ds(q + D_SECOND, size), :] * mask(3, q, size))
        low, high = sides[::-1] if back else sides
        return jnp.concatenate([low, field[pl.ds(q, size), :], high], 1)

    def first(q, size):
        x = near(f32, fb[pl.ds(q, size), :], q, size, False)
        act[pl.ds(q, size), :] = jnp.maximum(dot(x, w1[...]), 0.0).astype(BF)

    def second(q, size, targets):
        y = far(act, q, size, False)
        h = (f32[pl.ds(q, size), :] + dot(y, w2[...])).astype(BF)
        error = dot(wht[...], h, 1, 1) - targets
        gout = (error * scale).astype(BF)
        back = dot(gout, wht[...], 0, 0)
        gp2[pl.ds(q, size), :] = back.astype(BF)
        return h, error, gout, back

    def own(i):
        return (pl.multiple_of(i * step, step), pl.multiple_of(BASE + i * step, 16))

    def loop(body):
        lax.fori_loop(0, steps, lambda i, c: (body(*own(i)), c)[1], 0)

    last = BASE + rows
    widen(0, BASE)
    widen(last, BASE)
    loop(lambda t, q: widen(q, step))
    first(GAP, EDGE)
    first(last, EDGE)
    loop(lambda t, q: first(q, step))

    second(GAP, EDGE, tlo[...])
    second(last, EDGE, thi[...])

    def middle(t, q):
        h, error, gout, back = second(q, step, tgt[:, pl.ds(t, step)])
        hids[pl.ds(t, step), :] = h
        pltpu.make_async_copy(hids.at[pl.ds(t, step)], hid.at[pl.ds(t, step)], sem.at[3]).start()
        ghid[pl.ds(t, step), :] = back
        square = error * error
        part = square[:, 0:128]
        for j in range(1, step // 128):
            part = part + square[:, j * 128:(j + 1) * 128]
        err[...] += part
        ght[0:32, :] += dot(gout, h)

    loop(middle)

    def third(q, size):
        b = far(gp2, q, size, True)
        a = act[pl.ds(q, size), :]
        g = jnp.where(a > 0, dot(b, w2t[...]), 0.0)
        gp1[pl.ds(q, size), :] = g.astype(BF).astype(F32)
        return a, b

    third(EDGE, GAP)
    third(last, GAP)

    def outer(t, q):
        a, b = third(q, step)
        g2[...] += dot(a, b, 0, 0)

    loop(outer)

    def final(t, q):
        b = near(gp1, gp1[pl.ds(q, step), :].astype(BF), q, step, True)
        g1[...] += dot(fb[pl.ds(q, step), :], b, 0, 0)
        gfs[pl.ds(t, step), :] = (ghid[pl.ds(t, step), :] + dot(b, w1t[...])).astype(BF)
        pltpu.make_async_copy(gfs.at[pl.ds(t, step)], gfeat.at[pl.ds(t, step)], sem.at[4]).start()

    loop(final)
    gh[...] = ght[...].T
    pltpu.make_async_copy(hids, hid, sem.at[3]).wait()
    pltpu.make_async_copy(gfs, gfeat, sem.at[4]).wait()


def local(features, flo, fhi, seg, tgt, tlo, thi, w_first, w_second, wht, scale):
    rows, ch = features.shape
    total = rows + 2 * BASE
    vmem = pl.BlockSpec(memory_space=pltpu.VMEM)
    anys = pl.BlockSpec(memory_space=pl.ANY)
    traits = wht.shape[0]
    flops = 2 * rows * ch * ch * 20
    return pl.pallas_call(
        functools.partial(compute, rows, scale),
        out_shape=[
            jax.ShapeDtypeStruct((rows, ch), BF),
            jax.ShapeDtypeStruct((rows, ch), BF),
            jax.ShapeDtypeStruct((ch, 3 * ch), F32),
            jax.ShapeDtypeStruct((ch, 3 * ch), F32),
            jax.ShapeDtypeStruct((ch, 128), F32),
            jax.ShapeDtypeStruct((traits, 128), F32),
        ],
        in_specs=[anys] * 3 + [vmem] * 7,
        out_specs=[pl.BlockSpec(memory_space=pltpu.HBM)] * 2 + [vmem] * 4,
        scratch_shapes=[
            pltpu.VMEM((total, ch), BF),
            pltpu.VMEM((total, ch), F32),
            pltpu.VMEM((total, 128), F32),
            pltpu.VMEM((4, total, 128), BF),
            pltpu.VMEM((total, ch), BF),
            pltpu.VMEM((total, ch), BF),
            pltpu.VMEM((total, ch), F32),
            pltpu.VMEM((rows, ch), F32),
            pltpu.VMEM((3 * ch, ch), BF),
            pltpu.VMEM((3 * ch, ch), BF),
            pltpu.VMEM((128, ch), F32),
            pltpu.VMEM((rows, ch), BF),
            pltpu.VMEM((rows, ch), BF),
            pltpu.SemaphoreType.DMA((5,)),
        ],
        compiler_params=pltpu.CompilerParams(vmem_limit_bytes=56 * 2**20),
        cost_estimate=pl.CostEstimate(flops=flops, bytes_accessed=8 * rows * ch, transcendentals=0),
    )(features, flo, fhi, seg, tgt, tlo, thi, w_first, w_second, wht)


def total_kernel(h1, h2, hh, he, o1, o2, oh, oe, g1, g2, gh, err, lsem,
                 out1, in1, part1, out2, in2, part2, in3, out3, res, eout, ein, ez, ssem, rsem):
    me = lax.axis_index("tm")
    group = lax.axis_index("groups")
    core, x, z = lax.rem(me, 2), lax.rem(me // 2, 2), me // 4

    def at(zz, xx, cc):
        return (group, (zz * 2 + xx) * 2 + cc)

    other_core = at(z, x, 1 - core)
    other_x = at(z, 1 - x, core)
    others_z = [at(lax.rem(z + k, 4), x, core) for k in (1, 2, 3)]

    fetched = [pltpu.make_async_copy(src, dst, lsem.at[n])
               for n, (src, dst) in enumerate(((h2, g2), (h1, g1), (hh, gh), (he, err)))]
    for copy in fetched:
        copy.start()
    barrier = pltpu.get_barrier_semaphore()
    for peer in [other_core, other_x] + others_z:
        pl.semaphore_signal(barrier, inc=1, device_id=peer, device_id_type=MESH)
    pl.semaphore_wait(barrier, 5)

    count = [0]

    def send(src, dst, peer):
        n = count[0]
        count[0] += 1
        copy = pltpu.make_async_remote_copy(
            src_ref=src, dst_ref=dst, send_sem=ssem.at[n], recv_sem=rsem.at[n],
            device_id=peer, device_id_type=MESH)
        copy.start()
        return copy

    wide = g2.shape[1]
    half, quarter, mine = 128, 64, 16
    c0 = pl.multiple_of(core * half, half)
    c1 = pl.multiple_of((1 - core) * half, half)
    x0 = pl.multiple_of(x * quarter, quarter)
    x1 = pl.multiple_of((1 - x) * quarter, quarter)
    z0 = pl.multiple_of(z * mine, mine)

    part = wide // 2
    pieces = [(0, part), (part, part), (wide, part), (wide + part, part + 128)]

    def load(piece, start):
        left = (piece % 2) * part
        own = (g2 if piece < 2 else g1)[pl.ds(start, half), left:left + part]
        return own if piece < 3 else jnp.concatenate([own, gh[pl.ds(start, half), :]], 1)

    def cols(ref, piece):
        start, size = pieces[piece]
        return ref.at[:, start:start + size]

    def step1(p):
        start, size = pieces[p]
        out1[:, start:start + size] = load(p, c1).astype(BF)
        return send(cols(out1, p), cols(in1, p), other_core)

    def step2(p):
        start, size = pieces[p]
        part1[:, start:start + size] = load(p, c0) + in1[:, start:start + size].astype(F32)
        out2[:, start:start + size] = part1[pl.ds(x1, quarter), start:start + size].astype(BF)
        return send(cols(out2, p), cols(in2, p), other_x)

    def step3(p):
        start, size = pieces[p]
        part2[:, start:start + size] = (
            part1[pl.ds(x0, quarter), start:start + size] + in2[:, start:start + size].astype(F32))
        out3[:, start:start + size] = part2[:, start:start + size].astype(BF)
        copies = []
        for k in (1, 2, 3):
            to = pl.multiple_of(lax.rem(z + k, 4) * mine, mine)
            copies.append(send(out3.at[pl.ds(to, mine), start:start + size],
                               in3.at[k - 1, :, start:start + size], others_z[k - 1]))
        return copies

    home = pl.multiple_of(c0 + x0 + z0, mine)
    home_x = pl.multiple_of(c0 + x0, quarter)

    def step4(p):
        start, size = pieces[p]
        total = part2[pl.ds(z0, mine), start:start + size]
        for k in range(3):
            total = total + in3[k, :, start:start + size].astype(F32)
        res[pl.ds(home, mine), start:start + size] = total.astype(BF)
        spot = res.at[pl.ds(home, mine), start:start + size]
        return [send(spot, spot, others_z[k]) for k in range(3)]

    def step5(p):
        start, size = pieces[p]
        spot = res.at[pl.ds(home_x, quarter), start:start + size]
        return send(spot, spot, other_x)

    def step6(p):
        start, size = pieces[p]
        spot = res.at[pl.ds(c0, half), start:start + size]
        return send(spot, spot, other_core)

    def arrived(copies):
        for copy in copies if isinstance(copies, list) else [copies]:
            copy.wait()

    fetched[0].wait()
    flying = [step1(0), step1(1)]
    for copy in fetched[1:]:
        copy.wait()
    flying += [step1(2), step1(3)]
    eout[0] = err[...]
    error = send(eout.at[0], ein.at[0], other_core)
    for number, step in enumerate((step2, step3, step4, step5, step6)):
        for p in range(4):
            arrived(flying[p])
            flying[p] = step(p)
        if number == 0:
            error.wait()
            eout[1] = eout[0] + ein[0]
            error = send(eout.at[1], ein.at[1], other_x)
        elif number == 1:
            error.wait()
            ez[z] = eout[1] + ein[1]
            error = [send(ez.at[z], ez.at[z], peer) for peer in others_z]
        elif number == 2:
            arrived(error)
            oe[...] = ez[0] + ez[1] + ez[2] + ez[3]

    for p in range(4):
        arrived(flying[p])
        left = (p % 2) * part
        (o2 if p < 2 else o1)[:, left:left + part] = res[:, p * part:(p + 1) * part].astype(F32)
    oh[...] = res[:, 2 * wide:].astype(F32).T


def summed(g1, g2, gh, err):
    ch, wide = g1.shape
    every = 2 * wide + 128
    vmem = pl.BlockSpec(memory_space=pltpu.VMEM)
    return pl.pallas_call(
        total_kernel,
        out_shape=[
            jax.ShapeDtypeStruct((ch, wide), F32),
            jax.ShapeDtypeStruct((ch, wide), F32),
            jax.ShapeDtypeStruct((128, ch), F32),
            jax.ShapeDtypeStruct(err.shape, F32),
        ],
        in_specs=[pl.BlockSpec(memory_space=pltpu.HBM)] * 4,
        out_specs=[vmem] * 4,
        scratch_shapes=[
            pltpu.VMEM((ch, wide), F32), pltpu.VMEM((ch, wide), F32), pltpu.VMEM((ch, 128), F32),
            pltpu.VMEM(err.shape, F32), pltpu.SemaphoreType.DMA((4,)),
            pltpu.VMEM((128, every), BF), pltpu.VMEM((128, every), BF), pltpu.VMEM((128, every), F32),
            pltpu.VMEM((64, every), BF), pltpu.VMEM((64, every), BF), pltpu.VMEM((64, every), F32),
            pltpu.VMEM((3, 16, every), BF), pltpu.VMEM((64, every), BF), pltpu.VMEM((ch, every), BF),
            pltpu.VMEM((2,) + err.shape, F32), pltpu.VMEM((2,) + err.shape, F32),
            pltpu.VMEM((4,) + err.shape, F32),
            pltpu.SemaphoreType.DMA((45,)), pltpu.SemaphoreType.DMA((45,)),
        ],
        compiler_params=pltpu.CompilerParams(
            collective_id=1, has_side_effects=True, vmem_limit_bytes=32 * 2**20),
    )(g1, g2, gh, err)


def halo_kernel(count, feat, seg, tgt, flo, fhi, tlo, thi, both, inlo, inhi, tinlo, tinhi, slo, shi, ssem, rsem):
    me = lax.axis_index("tm")
    group = lax.axis_index("groups")
    right = (group, lax.rem(me + 1, count))
    left = (group, lax.rem(me + count - 1, count))
    barrier = pltpu.get_barrier_semaphore()
    for peer in (left, right):
        pl.semaphore_signal(barrier, inc=1, device_id=peer, device_id_type=MESH)
    pl.semaphore_wait(barrier, 2)
    rows, lines = feat.shape[0], seg.shape[0]
    plan = [
        (feat.at[pl.ds(rows - HALO, HALO)], inlo, right),
        (feat.at[pl.ds(0, HALO)], inhi, left),
        (tgt.at[:, pl.ds(rows - EDGE, EDGE)], tinlo, right),
        (tgt.at[:, pl.ds(0, EDGE)], tinhi, left),
        (seg.at[pl.ds(lines - 8, 8)], slo, right),
        (seg.at[pl.ds(0, 8)], shi, left),
    ]
    copies = [
        pltpu.make_async_remote_copy(
            src_ref=src, dst_ref=dst, send_sem=ssem.at[n], recv_sem=rsem.at[n],
            device_id=peer, device_id_type=MESH)
        for n, (src, dst, peer) in enumerate(plan)
    ]
    for copy in copies:
        copy.start()
    both[1:1 + lines, :] = seg[...] + 1
    for copy in copies:
        copy.wait()
    flo[...] = inlo[...]
    fhi[...] = inhi[...]
    tlo[...] = tinlo[...]
    thi[...] = tinhi[...]
    both[0:1, :] = jnp.where(me == 0, 0, slo[7:8, :] + 1)
    both[1 + lines:2 + lines, :] = jnp.where(me == count - 1, 0, shi[0:1, :] + 1)


def halos(features, segment, tgt):
    ch, traits = features.shape[1], tgt.shape[0]
    lines = segment.shape[0] // 128
    vmem = pl.BlockSpec(memory_space=pltpu.VMEM)
    hbm = pl.BlockSpec(memory_space=pltpu.HBM)
    shapes = [((HALO, ch), BF)] * 2 + [((traits, EDGE), F32)] * 2
    return pl.pallas_call(
        functools.partial(halo_kernel, lax.axis_size("tm")),
        out_shape=[jax.ShapeDtypeStruct(*s) for s in shapes + [((lines + 2, 128), jnp.int32)]],
        in_specs=[hbm, vmem, hbm],
        out_specs=[vmem] * 5,
        scratch_shapes=[pltpu.VMEM(*s) for s in shapes + [((8, 128), jnp.int32)] * 2] + [
            pltpu.SemaphoreType.DMA((6,)), pltpu.SemaphoreType.DMA((6,))],
        compiler_params=pltpu.CompilerParams(collective_id=2, has_side_effects=True),
    )(features, segment.reshape(-1, 128), tgt)


def shards(features, segment, w_first, w_second, w_head, targets):
    rows, ch = features.shape
    count = lax.axis_size("tm")
    every = rows * count
    traits = w_head.shape[1]
    tgt, wht = targets.T, w_head.T
    flo, fhi, tlo, thi, seg = halos(features, segment, tgt)
    hidden, gfeat, g1, g2, gh, err = local(
        features, flo, fhi, seg, tgt, tlo, thi, w_first, w_second, wht, 1.0 / every**0.5)
    if count == 16 and ch == 256:
        g1, g2, ght, err = summed(g1, g2, gh, err)
    else:
        g1, g2, gh, err = lax.psum((g1, g2, gh, err), "tm")
        ght = gh.T
    loss = jnp.reshape(jnp.sum(err) / (every * traits), (1,))

    def taps(g):
        return jnp.concatenate([g[:, k * ch:(k + 1) * ch] for k in range(3)], 0)

    return hidden, gfeat, taps(g1), taps(g2), ght[:traits].T, loss


def solution(mesh):
    return jax.shard_map(
        shards,
        mesh=mesh,
        in_specs=(
            P(("groups", "tm"), None),
            P(("groups", "tm")),
            P(),
            P(),
            P(),
            P(("groups", "tm"), None),
        ),
        out_specs=(
            P(("groups", "tm"), None),
            P(("groups", "tm"), None),
            P("groups", None),
            P("groups", None),
            P("groups", None),
            P("groups"),
        ),
        check_vma=False,
    )
```

```python
import functools

import jax
import jax.numpy as jnp
from jax import lax
from jax.experimental import pallas as pl
from jax.experimental.pallas import tpu as pltpu
from jax.sharding import PartitionSpec as P

D_FIRST = 4
D_SECOND = 16
EDGE = 128
GAP = 16
BASE = EDGE + GAP
HALO = 64
BF, F32 = jnp.bfloat16, jnp.float32
MESH = pl.DeviceIdType.MESH


def dot(a, b, ca=1, cb=0):
    return lax.dot_general(a, b, (((ca,), (cb,)), ((), ())), preferred_element_type=F32)


def compute(rows, scale, feat, flo, fhi, seg, tgt, tlo, thi, w1, w2, wht,
            hid, gfeat, g1, g2, gh, err,
            fb, f32, segc, msk, act, gp2, gp1, ghid, w1t, w2t, ght, hids, gfs, sem):
    ch = w1.shape[1]
    total = rows + 2 * BASE
    step = min(1024, rows)
    steps = rows // step

    copies = [
        pltpu.make_async_copy(feat, fb.at[pl.ds(BASE, rows)], sem.at[0]),
        pltpu.make_async_copy(flo, fb.at[pl.ds(BASE - HALO, HALO)], sem.at[1]),
        pltpu.make_async_copy(fhi, fb.at[pl.ds(BASE + rows, HALO)], sem.at[2]),
    ]
    for copy in copies:
        copy.start()

    diagonal = lax.broadcasted_iota(jnp.int32, (128, 128), 0) == lax.broadcasted_iota(
        jnp.int32, (128, 128), 1)
    ones = jnp.ones((256, 128), BF)

    def column(i, _):
        row = jnp.broadcast_to(seg[i:i + 1, :], (128, 128))
        low = row & 255
        high = row - low
        both = jnp.concatenate([jnp.where(diagonal, low, 0), jnp.where(diagonal, high, 0)], 1)
        segc[pl.ds(GAP + i * 128, 128), :] = dot(both.astype(F32).astype(BF), ones)
        return 0

    for i in range(seg.shape[0]):
        column(i, 0)
    segc[0:GAP, :] = jnp.full((GAP, 128), -1.0, F32)
    segc[total - GAP:total, :] = jnp.full((GAP, 128), -1.0, F32)

    block = 2 * 128 if seg.shape[0] % 2 == 0 else 128

    def masks(i, _):
        q = pl.multiple_of(GAP + i * block, 16)
        around = segc.at[pl.ds(q - GAP, block + 2 * GAP), :]
        center = around[GAP:GAP + block, :]
        for n, off in enumerate((-D_FIRST, D_FIRST, -D_SECOND, D_SECOND)):
            same = around[GAP + off:GAP + off + block, :] == center
            msk[n, pl.ds(q, block), :] = jnp.where(same, 1.0, 0.0).astype(BF)
        return 0

    lax.fori_loop(0, seg.shape[0] * 128 // block, masks, 0)

    for k in range(3):
        w1t[k * ch:(k + 1) * ch, :] = w1[k * ch:(k + 1) * ch, :].T
        w2t[k * ch:(k + 1) * ch, :] = w2[k * ch:(k + 1) * ch, :].T
    for scratch, edge, kind in ((act, GAP, BF), (gp2, GAP, BF), (fb, BASE - HALO, BF), (gp1, EDGE, F32)):
        zero = jnp.zeros((edge, ch), kind)
        scratch[0:edge, :] = zero
        scratch[total - edge:total, :] = zero
    g1[...] = jnp.zeros_like(g1)
    g2[...] = jnp.zeros_like(g2)
    ght[...] = jnp.zeros_like(ght)
    err[...] = jnp.zeros_like(err)
    for copy in copies:
        copy.wait()

    def widen(q, size):
        f32[pl.ds(q, size), :] = fb[pl.ds(q, size), :].astype(F32)

    def mask(n, q, size):
        m = msk[n, pl.ds(q, size), :]
        return jnp.concatenate([m] * (ch // 128), 1)

    def near(wide, exact, q, size, back):
        around = wide.at[pl.ds(q - 8, size + 16), :]
        sides = (around[8 - D_FIRST:8 - D_FIRST + size, :].astype(BF) * mask(0, q, size),
                 around[8 + D_FIRST:8 + D_FIRST + size, :].astype(BF) * mask(1, q, size))
        low, high = sides[::-1] if back else sides
        return jnp.concatenate([low, exact, high], 1)

    def far(field, q, size, back):
        sides = (field[pl.ds(q - D_SECOND, size), :] * mask(2, q, size),
                 field[pl.ds(q + D_SECOND, size), :] * mask(3, q, size))
        low, high = sides[::-1] if back else sides
        return jnp.concatenate([low, field[pl.ds(q, size), :], high], 1)

    def first(q, size):
        x = near(f32, fb[pl.ds(q, size), :], q, size, False)
        act[pl.ds(q, size), :] = jnp.maximum(dot(x, w1[...]), 0.0).astype(BF)

    def second(q, size, targets):
        y = far(act, q, size, False)
        h = (f32[pl.ds(q, size), :] + dot(y, w2[...])).astype(BF)
        error = dot(wht[...], h, 1, 1) - targets
        gout = (error * scale).astype(BF)
        back = dot(gout, wht[...], 0, 0)
        gp2[pl.ds(q, size), :] = back.astype(BF)
        return h, error, gout, back

    def own(i):
        return (pl.multiple_of(i * step, step), pl.multiple_of(BASE + i * step, 16))

    def loop(body):
        lax.fori_loop(0, steps, lambda i, c: (body(*own(i)), c)[1], 0)

    last = BASE + rows
    widen(0, BASE)
    widen(last, BASE)
    loop(lambda t, q: widen(q, step))
    first(GAP, EDGE)
    first(last, EDGE)
    loop(lambda t, q: first(q, step))

    second(GAP, EDGE, tlo[...])
    second(last, EDGE, thi[...])

    def middle(t, q):
        h, error, gout, back = second(q, step, tgt[:, pl.ds(t, step)])
        hids[pl.ds(t, step), :] = h
        pltpu.make_async_copy(hids.at[pl.ds(t, step)], hid.at[pl.ds(t, step)], sem.at[3]).start()
        ghid[pl.ds(t, step), :] = back
        square = error * error
        part = square[:, 0:128]
        for j in range(1, step // 128):
            part = part + square[:, j * 128:(j + 1) * 128]
        err[...] += part
        ght[0:32, :] += dot(gout, h)

    loop(middle)

    def third(q, size):
        b = far(gp2, q, size, True)
        a = act[pl.ds(q, size), :]
        g = jnp.where(a > 0, dot(b, w2t[...]), 0.0)
        gp1[pl.ds(q, size), :] = g.astype(BF).astype(F32)
        return a, b

    third(EDGE, GAP)
    third(last, GAP)

    def outer(t, q):
        a, b = third(q, step)
        g2[...] += dot(a, b, 0, 0)

    loop(outer)

    def final(t, q):
        b = near(gp1, gp1[pl.ds(q, step), :].astype(BF), q, step, True)
        g1[...] += dot(fb[pl.ds(q, step), :], b, 0, 0)
        gfs[pl.ds(t, step), :] = (ghid[pl.ds(t, step), :] + dot(b, w1t[...])).astype(BF)
        pltpu.make_async_copy(gfs.at[pl.ds(t, step)], gfeat.at[pl.ds(t, step)], sem.at[4]).start()

    loop(final)
    gh[...] = ght[...].T
    pltpu.make_async_copy(hids, hid, sem.at[3]).wait()
    pltpu.make_async_copy(gfs, gfeat, sem.at[4]).wait()


def local(features, flo, fhi, seg, tgt, tlo, thi, w_first, w_second, wht, scale):
    rows, ch = features.shape
    total = rows + 2 * BASE
    vmem = pl.BlockSpec(memory_space=pltpu.VMEM)
    anys = pl.BlockSpec(memory_space=pl.ANY)
    traits = wht.shape[0]
    flops = 2 * rows * ch * ch * 20
    return pl.pallas_call(
        functools.partial(compute, rows, scale),
        out_shape=[
            jax.ShapeDtypeStruct((rows, ch), BF),
            jax.ShapeDtypeStruct((rows, ch), BF),
            jax.ShapeDtypeStruct((ch, 3 * ch), F32),
            jax.ShapeDtypeStruct((ch, 3 * ch), F32),
            jax.ShapeDtypeStruct((ch, 128), F32),
            jax.ShapeDtypeStruct((traits, 128), F32),
        ],
        in_specs=[anys] * 3 + [vmem] * 7,
        out_specs=[pl.BlockSpec(memory_space=pltpu.HBM)] * 2 + [vmem] * 4,
        scratch_shapes=[
            pltpu.VMEM((total, ch), BF),
            pltpu.VMEM((total, ch), F32),
            pltpu.VMEM((total, 128), F32),
            pltpu.VMEM((4, total, 128), BF),
            pltpu.VMEM((total, ch), BF),
            pltpu.VMEM((total, ch), BF),
            pltpu.VMEM((total, ch), F32),
            pltpu.VMEM((rows, ch), F32),
            pltpu.VMEM((3 * ch, ch), BF),
            pltpu.VMEM((3 * ch, ch), BF),
            pltpu.VMEM((128, ch), F32),
            pltpu.VMEM((rows, ch), BF),
            pltpu.VMEM((rows, ch), BF),
            pltpu.SemaphoreType.DMA((5,)),
        ],
        compiler_params=pltpu.CompilerParams(vmem_limit_bytes=62 * 2**20),
        cost_estimate=pl.CostEstimate(flops=flops, bytes_accessed=8 * rows * ch, transcendentals=0),
    )(features, flo, fhi, seg, tgt, tlo, thi, w_first, w_second, wht)


def total_kernel(share, h1, h2, hh, he, o1, o2, oh, oe, g1, g2, gh, err, lsem,
                 out1, in1, part1, out2, in2, part2, in3, out3, res, eout, ein, ez, ssem, rsem):
    me = lax.axis_index("tm")
    group = lax.axis_index("groups")
    core, x, z = lax.rem(me, 2), lax.rem(me // 2, 2), me // 4

    def at(zz, xx, cc):
        return (group, (zz * 2 + xx) * 2 + cc)

    other_core = at(z, x, 1 - core)
    other_x = at(z, 1 - x, core)
    others_z = [at(lax.rem(z + k, 4), x, core) for k in (1, 2, 3)]

    fetched = [pltpu.make_async_copy(src, dst, lsem.at[n])
               for n, (src, dst) in enumerate(((h2, g2), (h1, g1), (hh, gh), (he, err)))]
    for copy in fetched:
        copy.start()
    barrier = pltpu.get_barrier_semaphore()
    for peer in [other_core, other_x] + others_z:
        pl.semaphore_signal(barrier, inc=1, device_id=peer, device_id_type=MESH)
    pl.semaphore_wait(barrier, 5)

    count = [0]

    def send(src, dst, peer):
        n = count[0]
        count[0] += 1
        copy = pltpu.make_async_remote_copy(
            src_ref=src, dst_ref=dst, send_sem=ssem.at[n], recv_sem=rsem.at[n],
            device_id=peer, device_id_type=MESH)
        copy.start()
        return copy

    wide = g2.shape[1]
    half, quarter, mine = 128, 64, 16
    c0 = pl.multiple_of(core * half, half)
    c1 = pl.multiple_of((1 - core) * half, half)
    x0 = pl.multiple_of(x * quarter, quarter)
    x1 = pl.multiple_of((1 - x) * quarter, quarter)
    z0 = pl.multiple_of(z * mine, mine)

    part = wide // 2
    pieces = [(0, part), (part, part), (wide, part), (wide + part, part + 128)]

    def load(piece, start):
        left = (piece % 2) * part
        own = (g2 if piece < 2 else g1)[pl.ds(start, half), left:left + part]
        return own if piece < 3 else jnp.concatenate([own, gh[pl.ds(start, half), :]], 1)

    def cols(ref, piece):
        start, size = pieces[piece]
        return ref.at[:, start:start + size]

    def step1(p):
        start, size = pieces[p]
        out1[:, start:start + size] = load(p, c1).astype(BF)
        return send(cols(out1, p), cols(in1, p), other_core)

    def step2(p):
        start, size = pieces[p]
        part1[:, start:start + size] = load(p, c0) + in1[:, start:start + size].astype(F32)
        out2[:, start:start + size] = part1[pl.ds(x1, quarter), start:start + size].astype(BF)
        return send(cols(out2, p), cols(in2, p), other_x)

    def step3(p):
        start, size = pieces[p]
        part2[:, start:start + size] = (
            part1[pl.ds(x0, quarter), start:start + size] + in2[:, start:start + size].astype(F32))
        out3[:, start:start + size] = part2[:, start:start + size].astype(BF)
        copies = []
        for k in (1, 2, 3):
            to = pl.multiple_of(lax.rem(z + k, 4) * mine, mine)
            copies.append(send(out3.at[pl.ds(to, mine), start:start + size],
                               in3.at[k - 1, :, start:start + size], others_z[k - 1]))
        return copies

    home = pl.multiple_of(c0 + x0 + z0, mine)
    home_x = pl.multiple_of(c0 + x0, quarter)

    def step4(p):
        start, size = pieces[p]
        total = part2[pl.ds(z0, mine), start:start + size]
        for k in range(3):
            total = total + in3[k, :, start:start + size].astype(F32)
        res[pl.ds(home, mine), start:start + size] = total.astype(BF)
        spot = res.at[pl.ds(home, mine), start:start + size]
        return [send(spot, spot, others_z[k]) for k in range(3)]

    def step5(p):
        start, size = pieces[p]
        spot = res.at[pl.ds(home_x, quarter), start:start + size]
        return send(spot, spot, other_x)

    def step6(p):
        start, size = pieces[p]
        spot = res.at[pl.ds(c0, half), start:start + size]
        return send(spot, spot, other_core)

    def arrived(copies):
        for copy in copies if isinstance(copies, list) else [copies]:
            copy.wait()

    fetched[0].wait()
    flying = [step1(0), step1(1)]
    for copy in fetched[1:]:
        copy.wait()
    flying += [step1(2), step1(3)]
    eout[0] = err[...]
    error = send(eout.at[0], ein.at[0], other_core)
    for number, step in enumerate((step2, step3, step4, step5, step6)):
        for p in range(4):
            arrived(flying[p])
            flying[p] = step(p)
        if number == 0:
            error.wait()
            eout[1] = eout[0] + ein[0]
            error = send(eout.at[1], ein.at[1], other_x)
        elif number == 1:
            error.wait()
            ez[z] = eout[1] + ein[1]
            error = [send(ez.at[z], ez.at[z], peer) for peer in others_z]
        elif number == 2:
            arrived(error)
            every = jnp.sum(ez[0] + ez[1] + ez[2] + ez[3], axis=(0, 1), keepdims=True)
            oe[...] = jnp.broadcast_to(every * share, oe.shape)

    for p in range(4):
        arrived(flying[p])
        left = (p % 2) * part
        (o2 if p < 2 else o1)[:, left:left + part] = res[:, p * part:(p + 1) * part].astype(F32)
    oh[...] = res[:, 2 * wide:].astype(F32).T


def summed(g1, g2, gh, err, share):
    ch, wide = g1.shape
    every = 2 * wide + 128
    vmem = pl.BlockSpec(memory_space=pltpu.VMEM)
    return pl.pallas_call(
        functools.partial(total_kernel, share),
        out_shape=[
            jax.ShapeDtypeStruct((ch, wide), F32),
            jax.ShapeDtypeStruct((ch, wide), F32),
            jax.ShapeDtypeStruct((128, ch), F32),
            jax.ShapeDtypeStruct((8, 128), F32),
        ],
        in_specs=[pl.BlockSpec(memory_space=pltpu.HBM)] * 4,
        out_specs=[vmem] * 4,
        scratch_shapes=[
            pltpu.VMEM((ch, wide), F32), pltpu.VMEM((ch, wide), F32), pltpu.VMEM((ch, 128), F32),
            pltpu.VMEM(err.shape, F32), pltpu.SemaphoreType.DMA((4,)),
            pltpu.VMEM((128, every), BF), pltpu.VMEM((128, every), BF), pltpu.VMEM((128, every), F32),
            pltpu.VMEM((64, every), BF), pltpu.VMEM((64, every), BF), pltpu.VMEM((64, every), F32),
            pltpu.VMEM((3, 16, every), BF), pltpu.VMEM((64, every), BF), pltpu.VMEM((ch, every), BF),
            pltpu.VMEM((2,) + err.shape, F32), pltpu.VMEM((2,) + err.shape, F32),
            pltpu.VMEM((4,) + err.shape, F32),
            pltpu.SemaphoreType.DMA((45,)), pltpu.SemaphoreType.DMA((45,)),
        ],
        compiler_params=pltpu.CompilerParams(
            collective_id=1, has_side_effects=True, vmem_limit_bytes=62 * 2**20),
    )(g1, g2, gh, err)


def halo_kernel(count, feat, seg, tgt, flo, fhi, tlo, thi, both, inlo, inhi, tinlo, tinhi, slo, shi, ssem, rsem):
    me = lax.axis_index("tm")
    group = lax.axis_index("groups")
    right = (group, lax.rem(me + 1, count))
    left = (group, lax.rem(me + count - 1, count))
    barrier = pltpu.get_barrier_semaphore()
    for peer in (left, right):
        pl.semaphore_signal(barrier, inc=1, device_id=peer, device_id_type=MESH)
    pl.semaphore_wait(barrier, 2)
    rows, lines = feat.shape[0], seg.shape[0]
    plan = [
        (feat.at[pl.ds(rows - HALO, HALO)], inlo, right),
        (feat.at[pl.ds(0, HALO)], inhi, left),
        (tgt.at[:, pl.ds(rows - EDGE, EDGE)], tinlo, right),
        (tgt.at[:, pl.ds(0, EDGE)], tinhi, left),
        (seg.at[pl.ds(lines - 8, 8)], slo, right),
        (seg.at[pl.ds(0, 8)], shi, left),
    ]
    copies = [
        pltpu.make_async_remote_copy(
            src_ref=src, dst_ref=dst, send_sem=ssem.at[n], recv_sem=rsem.at[n],
            device_id=peer, device_id_type=MESH)
        for n, (src, dst, peer) in enumerate(plan)
    ]
    for copy in copies:
        copy.start()
    both[1:1 + lines, :] = seg[...] + 1
    for copy in copies:
        copy.wait()
    flo[...] = inlo[...]
    fhi[...] = inhi[...]
    tlo[...] = tinlo[...]
    thi[...] = tinhi[...]
    both[0:1, :] = jnp.where(me == 0, 0, slo[7:8, :] + 1)
    both[1 + lines:2 + lines, :] = jnp.where(me == count - 1, 0, shi[0:1, :] + 1)


def halos(features, segment, tgt):
    ch, traits = features.shape[1], tgt.shape[0]
    lines = segment.shape[0] // 128
    vmem = pl.BlockSpec(memory_space=pltpu.VMEM)
    hbm = pl.BlockSpec(memory_space=pltpu.HBM)
    shapes = [((HALO, ch), BF)] * 2 + [((traits, EDGE), F32)] * 2
    return pl.pallas_call(
        functools.partial(halo_kernel, lax.axis_size("tm")),
        out_shape=[jax.ShapeDtypeStruct(*s) for s in shapes + [((lines + 2, 128), jnp.int32)]],
        in_specs=[hbm, vmem, hbm],
        out_specs=[vmem] * 5,
        scratch_shapes=[pltpu.VMEM(*s) for s in shapes + [((8, 128), jnp.int32)] * 2] + [
            pltpu.SemaphoreType.DMA((6,)), pltpu.SemaphoreType.DMA((6,))],
        compiler_params=pltpu.CompilerParams(collective_id=2, has_side_effects=True),
    )(features, segment.reshape(-1, 128), tgt)


def shards(features, segment, w_first, w_second, w_head, targets):
    rows, ch = features.shape
    count = lax.axis_size("tm")
    every = rows * count
    traits = w_head.shape[1]
    tgt, wht = targets.T, w_head.T
    flo, fhi, tlo, thi, seg = halos(features, segment, tgt)
    hidden, gfeat, g1, g2, gh, err = local(
        features, flo, fhi, seg, tgt, tlo, thi, w_first, w_second, wht, 1.0 / every**0.5)
    if count == 16 and ch == 256:
        g1, g2, ght, mean = summed(g1, g2, gh, err, 1.0 / (every * traits))
        loss = mean[0, 0:1]
    else:
        g1, g2, gh, err = lax.psum((g1, g2, gh, err), "tm")
        ght = gh.T
        loss = jnp.reshape(jnp.sum(err) / (every * traits), (1,))

    def taps(g):
        return jnp.concatenate([g[:, k * ch:(k + 1) * ch] for k in range(3)], 0)

    return hidden, gfeat, taps(g1), taps(g2), ght[:traits].T, loss


def solution(mesh):
    return jax.shard_map(
        shards,
        mesh=mesh,
        in_specs=(
            P(("groups", "tm"), None),
            P(("groups", "tm")),
            P(),
            P(),
            P(),
            P(("groups", "tm"), None),
        ),
        out_specs=(
            P(("groups", "tm"), None),
            P(("groups", "tm"), None),
            P("groups", None),
            P("groups", None),
            P("groups", None),
            P("groups"),
        ),
        check_vma=False,
    )
```

```python
import functools

import jax
import jax.numpy as jnp
from jax import lax
from jax.experimental import pallas as pl
from jax.experimental.pallas import tpu as pltpu
from jax.sharding import PartitionSpec as P

D_FIRST = 4
D_SECOND = 16
EDGE = 128
GAP = 16
BASE = EDGE + GAP
HALO = 64
BF, F32 = jnp.bfloat16, jnp.float32
MESH = pl.DeviceIdType.MESH


def dot(a, b, ca=1, cb=0):
    return lax.dot_general(a, b, (((ca,), (cb,)), ((), ())), preferred_element_type=F32)


def compute(rows, scale, feat, flo, fhi, seg, tgt, tlo, thi, w1, w2, wht,
            hid, gfeat, g1, g2, gh, err,
            fb, f32, segc, msk, act, gp2, gp1, ghid, w1t, w2t, ght, hids, gfs, sem):
    ch = w1.shape[1]
    total = rows + 2 * BASE
    step = min(1024, rows)
    steps = rows // step

    copies = [
        pltpu.make_async_copy(feat, fb.at[pl.ds(BASE, rows)], sem.at[0]),
        pltpu.make_async_copy(flo, fb.at[pl.ds(BASE - HALO, HALO)], sem.at[1]),
        pltpu.make_async_copy(fhi, fb.at[pl.ds(BASE + rows, HALO)], sem.at[2]),
    ]
    for copy in copies:
        copy.start()

    diagonal = lax.broadcasted_iota(jnp.int32, (128, 128), 0) == lax.broadcasted_iota(
        jnp.int32, (128, 128), 1)
    ones = jnp.ones((256, 128), BF)

    def column(i, _):
        row = jnp.broadcast_to(seg[i:i + 1, :], (128, 128))
        low = row & 255
        high = row - low
        both = jnp.concatenate([jnp.where(diagonal, low, 0), jnp.where(diagonal, high, 0)], 1)
        segc[pl.ds(GAP + i * 128, 128), :] = dot(both.astype(F32).astype(BF), ones)
        return 0

    for i in range(seg.shape[0]):
        column(i, 0)
    segc[0:GAP, :] = jnp.full((GAP, 128), -1.0, F32)
    segc[total - GAP:total, :] = jnp.full((GAP, 128), -1.0, F32)

    block = 2 * 128 if seg.shape[0] % 2 == 0 else 128

    def masks(i, _):
        q = pl.multiple_of(GAP + i * block, 16)
        around = segc.at[pl.ds(q - GAP, block + 2 * GAP), :]
        center = around[GAP:GAP + block, :]
        for n, off in enumerate((-D_FIRST, D_FIRST, -D_SECOND, D_SECOND)):
            same = around[GAP + off:GAP + off + block, :] == center
            msk[n, pl.ds(q, block), :] = jnp.where(same, 1.0, 0.0).astype(BF)
        return 0

    lax.fori_loop(0, seg.shape[0] * 128 // block, masks, 0)

    for k in range(3):
        w1t[k * ch:(k + 1) * ch, :] = w1[k * ch:(k + 1) * ch, :].T
        w2t[k * ch:(k + 1) * ch, :] = w2[k * ch:(k + 1) * ch, :].T
    for scratch, edge, kind in ((act, GAP, BF), (gp2, GAP, BF), (fb, BASE - HALO, BF), (gp1, EDGE, F32)):
        zero = jnp.zeros((edge, ch), kind)
        scratch[0:edge, :] = zero
        scratch[total - edge:total, :] = zero
    g1[...] = jnp.zeros_like(g1)
    g2[...] = jnp.zeros_like(g2)
    ght[...] = jnp.zeros_like(ght)
    err[...] = jnp.zeros_like(err)
    for copy in copies:
        copy.wait()

    def widen(q, size):
        f32[pl.ds(q, size), :] = fb[pl.ds(q, size), :].astype(F32)

    def mask(n, q, size):
        m = msk[n, pl.ds(q, size), :]
        return jnp.concatenate([m] * (ch // 128), 1)

    def near(wide, exact, q, size, back):
        around = wide.at[pl.ds(q - 8, size + 16), :]
        sides = (around[8 - D_FIRST:8 - D_FIRST + size, :].astype(BF) * mask(0, q, size),
                 around[8 + D_FIRST:8 + D_FIRST + size, :].astype(BF) * mask(1, q, size))
        low, high = sides[::-1] if back else sides
        return jnp.concatenate([low, exact, high], 1)

    def far(field, q, size, back):
        sides = (field[pl.ds(q - D_SECOND, size), :] * mask(2, q, size),
                 field[pl.ds(q + D_SECOND, size), :] * mask(3, q, size))
        low, high = sides[::-1] if back else sides
        return jnp.concatenate([low, field[pl.ds(q, size), :], high], 1)

    def first(q, size):
        x = near(f32, fb[pl.ds(q, size), :], q, size, False)
        act[pl.ds(q, size), :] = jnp.maximum(dot(x, w1[...]), 0.0).astype(BF)

    def second(q, size, targets):
        y = far(act, q, size, False)
        h = (f32[pl.ds(q, size), :] + dot(y, w2[...])).astype(BF)
        error = dot(wht[...], h, 1, 1) - targets
        gout = (error * scale).astype(BF)
        back = dot(gout, wht[...], 0, 0)
        gp2[pl.ds(q, size), :] = back.astype(BF)
        return h, error, gout, back

    def own(i):
        return (pl.multiple_of(i * step, step), pl.multiple_of(BASE + i * step, 16))

    def loop(body):
        lax.fori_loop(0, steps, lambda i, c: (body(*own(i)), c)[1], 0)

    last = BASE + rows
    widen(0, BASE)
    widen(last, BASE)
    loop(lambda t, q: widen(q, step))
    first(GAP, EDGE)
    first(last, EDGE)
    loop(lambda t, q: first(q, step))

    second(GAP, EDGE, tlo[...])
    second(last, EDGE, thi[...])

    def middle(t, q):
        h, error, gout, back = second(q, step, tgt[:, pl.ds(t, step)])
        hids[pl.ds(t, step), :] = h
        pltpu.make_async_copy(hids.at[pl.ds(t, step)], hid.at[pl.ds(t, step)], sem.at[3]).start()
        ghid[pl.ds(t, step), :] = back
        square = error * error
        part = square[:, 0:128]
        for j in range(1, step // 128):
            part = part + square[:, j * 128:(j + 1) * 128]
        err[...] += part
        ght[0:32, :] += dot(gout, h)

    loop(middle)

    def third(q, size):
        b = far(gp2, q, size, True)
        a = act[pl.ds(q, size), :]
        g = jnp.where(a > 0, dot(b, w2t[...]), 0.0)
        gp1[pl.ds(q, size), :] = g.astype(BF).astype(F32)
        return a, b

    third(EDGE, GAP)
    third(last, GAP)

    def outer(t, q):
        a, b = third(q, step)
        g2[...] += dot(a, b, 0, 0)

    loop(outer)

    def final(t, q):
        b = near(gp1, gp1[pl.ds(q, step), :].astype(BF), q, step, True)
        g1[...] += dot(fb[pl.ds(q, step), :], b, 0, 0)
        gfs[pl.ds(t, step), :] = (ghid[pl.ds(t, step), :] + dot(b, w1t[...])).astype(BF)
        pltpu.make_async_copy(gfs.at[pl.ds(t, step)], gfeat.at[pl.ds(t, step)], sem.at[4]).start()

    loop(final)
    gh[...] = ght[...].T
    pltpu.make_async_copy(hids, hid, sem.at[3]).wait()
    pltpu.make_async_copy(gfs, gfeat, sem.at[4]).wait()


def local(features, flo, fhi, seg, tgt, tlo, thi, w_first, w_second, wht, scale):
    rows, ch = features.shape
    total = rows + 2 * BASE
    vmem = pl.BlockSpec(memory_space=pltpu.VMEM)
    anys = pl.BlockSpec(memory_space=pl.ANY)
    traits = wht.shape[0]
    flops = 2 * rows * ch * ch * 20
    return pl.pallas_call(
        functools.partial(compute, rows, scale),
        out_shape=[
            jax.ShapeDtypeStruct((rows, ch), BF),
            jax.ShapeDtypeStruct((rows, ch), BF),
            jax.ShapeDtypeStruct((ch, 3 * ch), F32),
            jax.ShapeDtypeStruct((ch, 3 * ch), F32),
            jax.ShapeDtypeStruct((ch, 128), F32),
            jax.ShapeDtypeStruct((traits, 128), F32),
        ],
        in_specs=[anys] * 3 + [vmem] * 7,
        out_specs=[pl.BlockSpec(memory_space=pltpu.HBM)] * 2 + [vmem] * 4,
        scratch_shapes=[
            pltpu.VMEM((total, ch), BF),
            pltpu.VMEM((total, ch), F32),
            pltpu.VMEM((total, 128), F32),
            pltpu.VMEM((4, total, 128), BF),
            pltpu.VMEM((total, ch), BF),
            pltpu.VMEM((total, ch), BF),
            pltpu.VMEM((total, ch), F32),
            pltpu.VMEM((rows, ch), F32),
            pltpu.VMEM((3 * ch, ch), BF),
            pltpu.VMEM((3 * ch, ch), BF),
            pltpu.VMEM((128, ch), F32),
            pltpu.VMEM((rows, ch), BF),
            pltpu.VMEM((rows, ch), BF),
            pltpu.SemaphoreType.DMA((5,)),
        ],
        compiler_params=pltpu.CompilerParams(vmem_limit_bytes=62 * 2**20),
        cost_estimate=pl.CostEstimate(flops=flops, bytes_accessed=8 * rows * ch, transcendentals=0),
    )(features, flo, fhi, seg, tgt, tlo, thi, w_first, w_second, wht)


def total_kernel(share, h1, h2, hh, he, ores, oe, g1, g2, gh, err, lsem,
                 out1, in1, part1, out2, in2, part2, in3, out3, res, eout, ein, ez, ssem, rsem):
    me = lax.axis_index("tm")
    group = lax.axis_index("groups")
    core, x, z = lax.rem(me, 2), lax.rem(me // 2, 2), me // 4

    def at(zz, xx, cc):
        return (group, (zz * 2 + xx) * 2 + cc)

    other_core = at(z, x, 1 - core)
    other_x = at(z, 1 - x, core)
    others_z = [at(lax.rem(z + k, 4), x, core) for k in (1, 2, 3)]

    fetched = [pltpu.make_async_copy(src, dst, lsem.at[n])
               for n, (src, dst) in enumerate(((h2, g2), (h1, g1), (hh, gh), (he, err)))]
    for copy in fetched:
        copy.start()
    barrier = pltpu.get_barrier_semaphore()
    for peer in [other_core, other_x] + others_z:
        pl.semaphore_signal(barrier, inc=1, device_id=peer, device_id_type=MESH)
    pl.semaphore_wait(barrier, 5)

    count = [0]

    def send(src, dst, peer):
        n = count[0]
        count[0] += 1
        copy = pltpu.make_async_remote_copy(
            src_ref=src, dst_ref=dst, send_sem=ssem.at[n], recv_sem=rsem.at[n],
            device_id=peer, device_id_type=MESH)
        copy.start()
        return copy

    wide = g2.shape[1]
    half, quarter, mine = 128, 64, 16
    c0 = pl.multiple_of(core * half, half)
    c1 = pl.multiple_of((1 - core) * half, half)
    x0 = pl.multiple_of(x * quarter, quarter)
    x1 = pl.multiple_of((1 - x) * quarter, quarter)
    z0 = pl.multiple_of(z * mine, mine)

    part = wide // 2
    pieces = [(0, part), (part, part), (wide, part), (wide + part, part + 128)]

    def load(piece, start):
        left = (piece % 2) * part
        own = (g2 if piece < 2 else g1)[pl.ds(start, half), left:left + part]
        return own if piece < 3 else jnp.concatenate([own, gh[pl.ds(start, half), :]], 1)

    def cols(ref, piece):
        start, size = pieces[piece]
        return ref.at[:, start:start + size]

    def step1(p):
        start, size = pieces[p]
        out1[:, start:start + size] = load(p, c1).astype(BF)
        return send(cols(out1, p), cols(in1, p), other_core)

    def step2(p):
        start, size = pieces[p]
        part1[:, start:start + size] = load(p, c0) + in1[:, start:start + size].astype(F32)
        out2[:, start:start + size] = part1[pl.ds(x1, quarter), start:start + size].astype(BF)
        return send(cols(out2, p), cols(in2, p), other_x)

    def step3(p):
        start, size = pieces[p]
        part2[:, start:start + size] = (
            part1[pl.ds(x0, quarter), start:start + size] + in2[:, start:start + size].astype(F32))
        out3[:, start:start + size] = part2[:, start:start + size].astype(BF)
        copies = []
        for k in (1, 2, 3):
            to = pl.multiple_of(lax.rem(z + k, 4) * mine, mine)
            copies.append(send(out3.at[pl.ds(to, mine), start:start + size],
                               in3.at[k - 1, :, start:start + size], others_z[k - 1]))
        return copies

    home = pl.multiple_of(c0 + x0 + z0, mine)
    home_x = pl.multiple_of(c0 + x0, quarter)

    def step4(p):
        start, size = pieces[p]
        total = part2[pl.ds(z0, mine), start:start + size]
        for k in range(3):
            total = total + in3[k, :, start:start + size].astype(F32)
        res[pl.ds(home, mine), start:start + size] = total.astype(BF)
        spot = res.at[pl.ds(home, mine), start:start + size]
        return [send(spot, spot, others_z[k]) for k in range(3)]

    def step5(p):
        start, size = pieces[p]
        spot = res.at[pl.ds(home_x, quarter), start:start + size]
        return send(spot, spot, other_x)

    def step6(p):
        start, size = pieces[p]
        spot = res.at[pl.ds(c0, half), start:start + size]
        return send(spot, spot, other_core)

    def arrived(copies):
        for copy in copies if isinstance(copies, list) else [copies]:
            copy.wait()

    fetched[0].wait()
    flying = [step1(0), step1(1)]
    for copy in fetched[1:]:
        copy.wait()
    flying += [step1(2), step1(3)]
    eout[0] = err[...]
    error = send(eout.at[0], ein.at[0], other_core)
    for number, step in enumerate((step2, step3, step4, step5, step6)):
        for p in range(4):
            arrived(flying[p])
            flying[p] = step(p)
        if number == 0:
            error.wait()
            eout[1] = eout[0] + ein[0]
            error = send(eout.at[1], ein.at[1], other_x)
        elif number == 1:
            error.wait()
            ez[z] = eout[1] + ein[1]
            error = [send(ez.at[z], ez.at[z], peer) for peer in others_z]
        elif number == 2:
            arrived(error)
            every = jnp.sum(ez[0] + ez[1] + ez[2] + ez[3], axis=(0, 1), keepdims=True)
            oe[...] = jnp.broadcast_to(every * share, oe.shape)

    for p in range(4):
        arrived(flying[p])
        start, size = pieces[p]
        ores[:, start:start + size] = res[:, start:start + size]


def spread_kernel(sums, mean, first, second, head, loss):
    ch, wide = sums.shape[0], first.shape[0]
    for k in range(3):
        second[k * ch:(k + 1) * ch, :] = sums[:, k * ch:(k + 1) * ch].astype(F32)
        first[k * ch:(k + 1) * ch, :] = sums[:, wide + k * ch:wide + (k + 1) * ch].astype(F32)
    head[...] = sums[:, 2 * wide:].astype(F32).T[0:head.shape[0], :]
    loss[0] = mean[0, 0]


def spread(sums, mean, traits):
    ch = sums.shape[0]
    wide = (sums.shape[1] - 128) // 2
    vmem = pl.BlockSpec(memory_space=pltpu.VMEM)
    smem = pl.BlockSpec(memory_space=pltpu.SMEM)
    return pl.pallas_call(
        spread_kernel,
        out_shape=[
            jax.ShapeDtypeStruct((wide, ch), F32),
            jax.ShapeDtypeStruct((wide, ch), F32),
            jax.ShapeDtypeStruct((traits, ch), F32),
            jax.ShapeDtypeStruct((1,), F32),
        ],
        in_specs=[vmem, smem],
        out_specs=[vmem, vmem, vmem, smem],
        compiler_params=pltpu.CompilerParams(vmem_limit_bytes=62 * 2**20),
    )(sums, mean)


def summed(g1, g2, gh, err, share):
    ch, wide = g1.shape
    every = 2 * wide + 128
    vmem = pl.BlockSpec(memory_space=pltpu.VMEM)
    return pl.pallas_call(
        functools.partial(total_kernel, share),
        out_shape=[
            jax.ShapeDtypeStruct((ch, every), BF),
            jax.ShapeDtypeStruct((8, 128), F32),
        ],
        in_specs=[pl.BlockSpec(memory_space=pltpu.HBM)] * 4,
        out_specs=[vmem] * 2,
        scratch_shapes=[
            pltpu.VMEM((ch, wide), F32), pltpu.VMEM((ch, wide), F32), pltpu.VMEM((ch, 128), F32),
            pltpu.VMEM(err.shape, F32), pltpu.SemaphoreType.DMA((4,)),
            pltpu.VMEM((128, every), BF), pltpu.VMEM((128, every), BF), pltpu.VMEM((128, every), F32),
            pltpu.VMEM((64, every), BF), pltpu.VMEM((64, every), BF), pltpu.VMEM((64, every), F32),
            pltpu.VMEM((3, 16, every), BF), pltpu.VMEM((64, every), BF), pltpu.VMEM((ch, every), BF),
            pltpu.VMEM((2,) + err.shape, F32), pltpu.VMEM((2,) + err.shape, F32),
            pltpu.VMEM((4,) + err.shape, F32),
            pltpu.SemaphoreType.DMA((45,)), pltpu.SemaphoreType.DMA((45,)),
        ],
        compiler_params=pltpu.CompilerParams(
            collective_id=1, has_side_effects=True, vmem_limit_bytes=62 * 2**20),
    )(g1, g2, gh, err)


def halo_kernel(count, feat, seg, tgt, flo, fhi, tlo, thi, both, inlo, inhi, tinlo, tinhi, slo, shi, ssem, rsem):
    me = lax.axis_index("tm")
    group = lax.axis_index("groups")
    right = (group, lax.rem(me + 1, count))
    left = (group, lax.rem(me + count - 1, count))
    barrier = pltpu.get_barrier_semaphore()
    for peer in (left, right):
        pl.semaphore_signal(barrier, inc=1, device_id=peer, device_id_type=MESH)
    pl.semaphore_wait(barrier, 2)
    rows, lines = feat.shape[0], seg.shape[0]
    plan = [
        (feat.at[pl.ds(rows - HALO, HALO)], inlo, right),
        (feat.at[pl.ds(0, HALO)], inhi, left),
        (tgt.at[:, pl.ds(rows - EDGE, EDGE)], tinlo, right),
        (tgt.at[:, pl.ds(0, EDGE)], tinhi, left),
        (seg.at[pl.ds(lines - 8, 8)], slo, right),
        (seg.at[pl.ds(0, 8)], shi, left),
    ]
    copies = [
        pltpu.make_async_remote_copy(
            src_ref=src, dst_ref=dst, send_sem=ssem.at[n], recv_sem=rsem.at[n],
            device_id=peer, device_id_type=MESH)
        for n, (src, dst, peer) in enumerate(plan)
    ]
    for copy in copies:
        copy.start()
    both[1:1 + lines, :] = seg[...] + 1
    for copy in copies:
        copy.wait()
    flo[...] = inlo[...]
    fhi[...] = inhi[...]
    tlo[...] = tinlo[...]
    thi[...] = tinhi[...]
    both[0:1, :] = jnp.where(me == 0, 0, slo[7:8, :] + 1)
    both[1 + lines:2 + lines, :] = jnp.where(me == count - 1, 0, shi[0:1, :] + 1)


def halos(features, segment, tgt):
    ch, traits = features.shape[1], tgt.shape[0]
    lines = segment.shape[0] // 128
    vmem = pl.BlockSpec(memory_space=pltpu.VMEM)
    hbm = pl.BlockSpec(memory_space=pltpu.HBM)
    shapes = [((HALO, ch), BF)] * 2 + [((traits, EDGE), F32)] * 2
    return pl.pallas_call(
        functools.partial(halo_kernel, lax.axis_size("tm")),
        out_shape=[jax.ShapeDtypeStruct(*s) for s in shapes + [((lines + 2, 128), jnp.int32)]],
        in_specs=[hbm, vmem, hbm],
        out_specs=[vmem] * 5,
        scratch_shapes=[pltpu.VMEM(*s) for s in shapes + [((8, 128), jnp.int32)] * 2] + [
            pltpu.SemaphoreType.DMA((6,)), pltpu.SemaphoreType.DMA((6,))],
        compiler_params=pltpu.CompilerParams(collective_id=2, has_side_effects=True),
    )(features, segment.reshape(-1, 128), tgt)


def shards(features, segment, w_first, w_second, w_head, targets):
    rows, ch = features.shape
    count = lax.axis_size("tm")
    every = rows * count
    traits = w_head.shape[1]
    tgt, wht = targets.T, w_head.T
    flo, fhi, tlo, thi, seg = halos(features, segment, tgt)
    hidden, gfeat, g1, g2, gh, err = local(
        features, flo, fhi, seg, tgt, tlo, thi, w_first, w_second, wht, 1.0 / every**0.5)
    if count == 16 and ch == 256:
        first, second, head, loss = spread(*summed(g1, g2, gh, err, 1.0 / (every * traits)), traits)
        return hidden, gfeat, first, second, head.T, loss

    def taps(g):
        return jnp.concatenate([g[:, k * ch:(k + 1) * ch] for k in range(3)], 0)

    g1, g2, gh, err = lax.psum((g1, g2, gh, err), "tm")
    loss = jnp.reshape(jnp.sum(err) / (every * traits), (1,))
    return hidden, gfeat, taps(g1), taps(g2), gh[:, :traits], loss


def solution(mesh):
    return jax.shard_map(
        shards,
        mesh=mesh,
        in_specs=(
            P(("groups", "tm"), None),
            P(("groups", "tm")),
            P(),
            P(),
            P(),
            P(("groups", "tm"), None),
        ),
        out_specs=(
            P(("groups", "tm"), None),
            P(("groups", "tm"), None),
            P("groups", None),
            P("groups", None),
            P("groups", None),
            P("groups"),
        ),
        check_vma=False,
    )
```
